32 devices in a mesh: ten: 16 (over z, x, core), fsdp: 2 (over y).
Axes of the slice: x: 2, y: 2, z: 4, core: 2. Of those that a mesh axis runs over, the one named last changes fastest.
Arguments:
- activations: bfloat16 [16, 32, 32, 1280], P('ten', 'fsdp'), may hold values from -6 to 6
- cotangent: bfloat16 [16, 32, 32, 1280], P('ten', 'fsdp'), may hold values from -6 to 6
- base_kernel: bfloat16 [3, 1280, 3, 1280], P(None, 'fsdp'), may hold values from -0.0546875 to 0.0546875
- down_table: bfloat16 [16, 3, 3, 32, 1280], P(None, None, None, 'fsdp', 'ten'), may hold values from -0.0546875 to 0.0546875
- up_table: bfloat16 [16, 32, 1280], P(None, None, 'ten'), may hold values from -1 to 1
- sample_tenant: int32 [16], P('ten'), may hold values from 0 to 15
- tenant_slot: int32 [16], replicated, may hold values from 0 to 15, each once
- timesteps: int32 [16], P('ten'), may hold values from 0 to 999
Outputs:
- block_out: bfloat16 [16, 32, 32, 1280], P('ten', 'fsdp')
- down_grad: bfloat16 [16, 3, 3, 32, 1280], P(None, None, None, 'fsdp', 'ten')
- up_grad: bfloat16 [16, 32, 1280], P(None, None, 'ten')
The draws below stay inside these ranges and needn't reach their ends.
All inputs are finite; a program needn't handle non-finite values.
Results may differ from the reference program's by a relative error of at most 0.0066.
Values may be sent and summed in bfloat16 or wider, within the bound.
A program may use at most 128 MiB of HBM per device.

```python
import math
import jax
import jax.numpy as jnp
import numpy as np
from jax import lax

C = 1280
R = 32
HH = 32
WW = 32
TENANTS = 16
SAMPLES = 16


def touch_ends(drawn, own_key, low, top_value):
    place = [jax.random.randint(jax.random.fold_in(own_key, axis), (), 0, length) for axis, length in enumerate(drawn.shape)]
    main_axis = drawn.shape.index(max(drawn.shape))
    next_to = place[:main_axis] + [(place[main_axis] + 1) % drawn.shape[main_axis]] + place[main_axis + 1:]
    return drawn.at[tuple(place)].set(low).at[tuple(next_to)].set(top_value)


def block_scale(stream_key, extent, pieces, smallest, largest):
    level = 1.0
    for dim, blocks in pieces:
        heights = jax.random.uniform(jax.random.fold_in(jax.random.fold_in(stream_key, 6), dim), (blocks,), jnp.float32, smallest / len(pieces), largest / len(pieces))
        level = level * jnp.repeat(jnp.exp(heights), extent[dim] // blocks).reshape((-1,) + (1,) * (len(extent) - 1 - dim))
    return level


def rank_table(count, lean):
    weights = [(1 << 20) // math.isqrt(rank ** lean) + 1 for rank in range(1, count + 1)]
    spread = 1 + sum(weights) // (1 << 30)
    return np.cumsum(np.array([max(1, weight // spread) for weight in weights]))


def ranked(stream_key, extent, number_of, skew):
    table = rank_table(number_of, skew)
    pick = jax.random.randint(jax.random.fold_in(stream_key, 1), extent, 0, int(table[number_of - 1]))
    rank = jnp.searchsorted(jnp.asarray(table, jnp.int32), pick, side="right")
    return jax.random.permutation(jax.random.fold_in(stream_key, 2), number_of)[rank].astype(jnp.int32)


def scatter_about(key, dims, spread, limit, cuts=(), kind=jnp.bfloat16):
    entries = jax.random.normal(key, dims, jnp.float32) * spread
    if len(cuts) > 0:
        entries = block_scale(key, dims, cuts, -0.22, 0.18) * entries
    return jnp.clip(entries, min=-limit, max=limit).astype(kind)


def setup_inputs(seed: int = 0) -> dict:
    keys = jax.random.split(jax.random.key(seed), 9)
    return {
        "activations": scatter_about(keys[0], (SAMPLES, HH, WW, C), 1.0, 6.0, ((0, 16), (1, 2))),
        "cotangent": scatter_about(keys[1], (SAMPLES, HH, WW, C), 1.0, 6.0, ((0, 16), (1, 2))),
        "base_kernel": scatter_about(keys[2], (3, C, 3, C), (9 * C) ** -0.5, 0.0546875, ((1, 2),)),
        "down_table": scatter_about(keys[3], (TENANTS, 3, 3, R, C), (9 * C) ** -0.5, 0.0546875, ((3, 2), (4, 16))),
        "up_table": scatter_about(keys[4], (TENANTS, R, C), R ** -0.5, 1.0, ((2, 16),)),
        "sample_tenant": touch_ends(ranked(keys[5], (SAMPLES,), TENANTS, 2), jax.random.fold_in(keys[5], 3), 0, TENANTS - 1).astype(jnp.int32),
        "tenant_slot": jax.random.permutation(keys[6], TENANTS).astype(jnp.int32),
        "timesteps": touch_ends(jax.random.randint(keys[7], (SAMPLES,), 0, 1000), jax.random.fold_in(keys[7], 1), 0, 999).astype(jnp.int32),
    }


def conv_same(field, kernel):
    return lax.conv_general_dilated(field, kernel, (1, 1), "SAME", dimension_numbers=("NHWC", "HWIO", "NHWC"), preferred_element_type=jnp.float32)


def slope_of(block, cotangent, weight):
    value = block.astype(jnp.float32)
    sigma = jax.nn.sigmoid(value)
    return (cotangent.astype(jnp.float32) * weight * sigma * (1.0 + value * (1.0 - sigma))).astype(jnp.bfloat16)


def reference(activations, cotangent, base_kernel, down_table, up_table, sample_tenant, tenant_slot, timesteps):
    cells = HH * WW
    kernel_hwio = jnp.transpose(base_kernel, (0, 2, 3, 1))

    def one_sample(index):
        field = lax.dynamic_slice_in_dim(activations, index, 1, 0)
        cot = lax.dynamic_slice_in_dim(cotangent, index, 1, 0)
        slot = tenant_slot[sample_tenant[index]]
        down = down_table[slot]
        up_fac = up_table[slot]
        base = conv_same(field, kernel_hwio).astype(jnp.bfloat16)
        low = conv_same(field, jnp.transpose(down, (0, 1, 3, 2))).astype(jnp.bfloat16).reshape(cells, R)
        block = (base.reshape(cells, C).astype(jnp.float32) + jnp.dot(low, up_fac, preferred_element_type=jnp.float32)).astype(jnp.bfloat16)
        weight = 1.0 / (1.0 + timesteps[index].astype(jnp.float32) / 250.0)
        slope = slope_of(block, cot.reshape(cells, C), weight)
        up_term = jnp.dot(low.T, slope, preferred_element_type=jnp.float32).astype(jnp.bfloat16)
        low_grad = jnp.dot(slope, up_fac.T, preferred_element_type=jnp.float32).astype(jnp.bfloat16)
        padded = jnp.pad(field[0], ((1, 1), (1, 1), (0, 0)))
        rows_list = []
        for tap_row in range(3):
            cols_list = []
            for tap_col in range(3):
                shifted = padded[tap_row:tap_row + HH, tap_col:tap_col + WW].reshape(cells, C)
                cols_list.append(jnp.dot(low_grad.T, shifted, preferred_element_type=jnp.float32))
            rows_list.append(jnp.stack(cols_list))
        down_term = jnp.stack(rows_list).astype(jnp.bfloat16)
        return block.reshape(HH, WW, C), down_term, up_term, slot

    blocks, down_terms, up_terms, slots = lax.map(one_sample, jnp.arange(SAMPLES, dtype=jnp.int32))
    down_sum = jnp.zeros((TENANTS, 3, 3, R, C), jnp.float32).at[slots].add(down_terms.astype(jnp.float32))
    up_sum = jnp.zeros((TENANTS, R, C), jnp.float32).at[slots].add(up_terms.astype(jnp.float32))
    return blocks, down_sum.astype(jnp.bfloat16), up_sum.astype(jnp.bfloat16)
```

```python
import jax
import jax.numpy as jnp
from jax import lax
from jax.sharding import PartitionSpec as P


def conv_same(field, kernel):
    return lax.conv_general_dilated(
        field,
        kernel,
        (1, 1),
        "SAME",
        dimension_numbers=("NHWC", "HWIO", "NHWC"),
        preferred_element_type=jnp.float32,
    )


def slope_of(block, cotangent, weight):
    value = block.astype(jnp.float32)
    sigma = jax.nn.sigmoid(value)
    return (cotangent.astype(jnp.float32) * weight * sigma * (1.0 + value * (1.0 - sigma))).astype(
        jnp.bfloat16
    )


def local(
    activations, cotangent, base_kernel, down_table, up_table, sample_tenant, tenant_slot, timesteps
):
    width = base_kernel.shape[1]
    kernel_hwio = jnp.transpose(base_kernel, (0, 2, 3, 1))
    ten_index = lax.axis_index("ten")
    fsdp_index = lax.axis_index("fsdp")
    tenants = down_table.shape[0]
    rank = up_table.shape[1]
    block_cols = down_table.shape[4]
    all_tenants = lax.all_gather(sample_tenant, "ten", axis=0, tiled=True)
    all_slots = tenant_slot[all_tenants]
    groups = all_slots.shape[0]
    picks = (all_slots[:, None] == jnp.arange(tenants, dtype=jnp.int32)[None, :]).astype(
        jnp.bfloat16
    )
    send_down = jnp.einsum(
        "dl,labkc->dabkc", picks, down_table, preferred_element_type=jnp.float32
    ).astype(jnp.bfloat16)
    send_up = jnp.einsum("dl,lkc->dkc", picks, up_table, preferred_element_type=jnp.float32).astype(
        jnp.bfloat16
    )
    send_up = send_up.reshape(groups, 1, 1, rank, block_cols)
    recv_down, recv_up = (
        lax.all_to_all(send_down, "ten", split_axis=0, concat_axis=4, tiled=True),
        lax.all_to_all(send_up, "ten", split_axis=0, concat_axis=4, tiled=True),
    )
    down_fac = recv_down[0]
    up_whole = recv_up[0, 0, 0]
    up_fac = lax.dynamic_slice_in_dim(up_whole, fsdp_index * width, width, 1)
    whole = lax.all_gather(activations, "fsdp", axis=1, tiled=True)
    height = whole.shape[1]
    breadth = whole.shape[2]
    cells = height * breadth
    base_part = conv_same(whole, kernel_hwio).astype(jnp.bfloat16)
    low_slice = conv_same(whole, jnp.transpose(down_fac, (0, 1, 3, 2))).astype(jnp.bfloat16)
    low = lax.all_gather(low_slice, "fsdp", axis=3, tiled=True).reshape(cells, rank)
    y_cols = (
        base_part.reshape(cells, width).astype(jnp.float32)
        + jnp.dot(low, up_fac, preferred_element_type=jnp.float32)
    ).astype(jnp.bfloat16)
    y_cols = y_cols.reshape(1, height, breadth, width)
    block_out = lax.all_to_all(y_cols, "fsdp", split_axis=1, concat_axis=3, tiled=True)
    weight = 1.0 / (1.0 + timesteps[0].astype(jnp.float32) / 250.0)
    slope = lax.all_to_all(
        slope_of(block_out, cotangent, weight), "fsdp", split_axis=3, concat_axis=1, tiled=True
    )
    slope = slope.reshape(cells, width)
    up_term = lax.dot_general(
        low, slope, (((0,), (0,)), ((), ())), preferred_element_type=jnp.float32
    ).astype(jnp.bfloat16)
    grad_part = lax.dot_general(
        slope, up_fac, (((1,), (1,)), ((), ())), preferred_element_type=jnp.float32
    )
    low_grad = lax.psum_scatter(grad_part, "fsdp", scatter_dimension=1, tiled=True).astype(
        jnp.bfloat16
    )
    padded = jnp.pad(whole[0], ((1, 1), (1, 1), (0, 0)))
    channels = whole.shape[3]
    rows_list = []
    for tap_row in range(3):
        cols_list = []
        for tap_col in range(3):
            shifted = padded[tap_row : tap_row + height, tap_col : tap_col + breadth].reshape(
                cells, channels
            )
            cols_list.append(
                lax.dot_general(
                    low_grad, shifted, (((0,), (0,)), ((), ())), preferred_element_type=jnp.float32
                )
            )
        rows_list.append(jnp.stack(cols_list))
    down_term = jnp.stack(rows_list).astype(jnp.bfloat16)
    up_all = lax.all_gather(up_term, "fsdp", axis=1, tiled=True)
    down_piece = lax.all_to_all(down_term[None], "ten", split_axis=4, concat_axis=0, tiled=True)
    up_piece = lax.all_to_all(up_all[None], "ten", split_axis=2, concat_axis=0, tiled=True)
    down_sum = jnp.einsum("dl,dabkc->labkc", picks, down_piece, preferred_element_type=jnp.float32)
    up_sum = jnp.einsum("dl,dkc->lkc", picks, up_piece, preferred_element_type=jnp.float32)
    return (block_out, down_sum.astype(jnp.bfloat16), up_sum.astype(jnp.bfloat16))


def solution(mesh):
    placed = (
        P("ten", "fsdp", None, None),
        P("ten", "fsdp", None, None),
        P(None, "fsdp", None, None),
        P(None, None, None, "fsdp", "ten"),
        P(None, None, "ten"),
        P("ten"),
        P(),
        P("ten"),
    )
    return jax.shard_map(
        local,
        mesh=mesh,
        in_specs=placed,
        out_specs=(
            P("ten", "fsdp", None, None),
            P(None, None, None, "fsdp", "ten"),
            P(None, None, "ten"),
        ),
        check_vma=False,
    )
```

```python
import functools

import jax
import jax.numpy as jnp
from jax import lax
from jax.experimental import pallas as pl
from jax.experimental.pallas import tpu as pltpu
from jax.sharding import PartitionSpec as P


def conv_same(field, kernel):
    return lax.conv_general_dilated(
        field,
        kernel,
        (1, 1),
        "SAME",
        dimension_numbers=("NHWC", "HWIO", "NHWC"),
        preferred_element_type=jnp.float32,
    )


def slope_of(block, cotangent, weight):
    value = block.astype(jnp.float32)
    sigma = jax.nn.sigmoid(value)
    return (cotangent.astype(jnp.float32) * weight * sigma * (1.0 + value * (1.0 - sigma))).astype(
        jnp.bfloat16
    )


def local(
    activations, cotangent, base_kernel, down_table, up_table, sample_tenant, tenant_slot, timesteps
):
    width = base_kernel.shape[1]
    kernel_hwio = jnp.transpose(base_kernel, (0, 2, 3, 1))
    ten_index = lax.axis_index("ten")
    fsdp_index = lax.axis_index("fsdp")
    tenants = down_table.shape[0]
    rank = up_table.shape[1]
    block_cols = down_table.shape[4]
    all_tenants = lax.all_gather(sample_tenant, "ten", axis=0, tiled=True)
    all_slots = tenant_slot[all_tenants]
    groups = all_slots.shape[0]
    picks = (all_slots[:, None] == jnp.arange(tenants, dtype=jnp.int32)[None, :]).astype(
        jnp.bfloat16
    )
    send_down = jnp.einsum(
        "dl,labkc->dabkc", picks, down_table, preferred_element_type=jnp.float32
    ).astype(jnp.bfloat16)
    send_up = jnp.einsum("dl,lkc->dkc", picks, up_table, preferred_element_type=jnp.float32).astype(
        jnp.bfloat16
    )
    send_up = send_up.reshape(groups, 1, 1, rank, block_cols)
    recv_down, recv_up = (
        lax.all_to_all(send_down, "ten", split_axis=0, concat_axis=4, tiled=True),
        lax.all_to_all(send_up, "ten", split_axis=0, concat_axis=4, tiled=True),
    )
    down_fac = recv_down[0]
    up_whole = recv_up[0, 0, 0]
    up_fac = lax.dynamic_slice_in_dim(up_whole, fsdp_index * width, width, 1)
    whole = lax.all_gather(activations, "fsdp", axis=1, tiled=True)
    height = whole.shape[1]
    breadth = whole.shape[2]
    cells = height * breadth
    base_part = conv_same(whole, kernel_hwio).astype(jnp.bfloat16)
    low_slice = conv_same(whole, jnp.transpose(down_fac, (0, 1, 3, 2))).astype(jnp.bfloat16)
    low = lax.all_gather(low_slice, "fsdp", axis=3, tiled=True).reshape(cells, rank)
    y_cols = (
        base_part.reshape(cells, width).astype(jnp.float32)
        + jnp.dot(low, up_fac, preferred_element_type=jnp.float32)
    ).astype(jnp.bfloat16)
    y_cols = y_cols.reshape(1, height, breadth, width)
    block_out = lax.all_to_all(y_cols, "fsdp", split_axis=1, concat_axis=3, tiled=True)
    weight = 1.0 / (1.0 + timesteps[0].astype(jnp.float32) / 250.0)
    slope = lax.all_to_all(
        slope_of(block_out, cotangent, weight), "fsdp", split_axis=3, concat_axis=1, tiled=True
    )
    slope = slope.reshape(cells, width)
    up_term = lax.dot_general(
        low, slope, (((0,), (0,)), ((), ())), preferred_element_type=jnp.float32
    ).astype(jnp.bfloat16)
    grad_part = lax.dot_general(
        slope, up_fac, (((1,), (1,)), ((), ())), preferred_element_type=jnp.float32
    )
    low_grad = lax.psum_scatter(grad_part, "fsdp", scatter_dimension=1, tiled=True).astype(
        jnp.bfloat16
    )
    padded = jnp.pad(whole[0], ((1, 1), (1, 1), (0, 0)))
    channels = whole.shape[3]
    rows_list = []
    for tap_row in range(3):
        cols_list = []
        for tap_col in range(3):
            shifted = padded[tap_row : tap_row + height, tap_col : tap_col + breadth].reshape(
                cells, channels
            )
            cols_list.append(
                lax.dot_general(
                    low_grad, shifted, (((0,), (0,)), ((), ())), preferred_element_type=jnp.float32
                )
            )
        rows_list.append(jnp.stack(cols_list))
    down_term = jnp.stack(rows_list).astype(jnp.bfloat16)
    up_all = lax.all_gather(up_term, "fsdp", axis=1, tiled=True)
    down_piece = lax.all_to_all(down_term[None], "ten", split_axis=4, concat_axis=0, tiled=True)
    up_piece = lax.all_to_all(up_all[None], "ten", split_axis=2, concat_axis=0, tiled=True)
    down_sum = jnp.einsum("dl,dabkc->labkc", picks, down_piece, preferred_element_type=jnp.float32)
    up_sum = jnp.einsum("dl,dkc->lkc", picks, up_piece, preferred_element_type=jnp.float32)
    return (block_out, down_sum.astype(jnp.bfloat16), up_sum.astype(jnp.bfloat16))


NT = (((1,), (1,)), ((), ()))
TN = (((0,), (0,)), ((), ()))
F32 = jnp.float32
BF16 = jnp.bfloat16


def core_kernel(
    act, cot, kern, df, up, wgt, out, down_out, up_out,
    field, kbuf, part, lown, lowp, bbuf, block, ysend, cotv, slope, lgt, lgall, taps, upp, upr,
    ksem, lsem, ssem, rsem, *, wide, chunk,
):
    y = lax.axis_index("fsdp")
    other = 1 - y
    peer = {"fsdp": other}
    cells, channels = act.shape
    width = kern.shape[1]
    half = df.shape[1]
    total = 2 * cells

    def rows(start, size):
        return pl.ds(pl.multiple_of(start, wide), size)

    ranks = pl.ds(pl.multiple_of(width + half * y, half), half)
    mine = wide + cells * y
    theirs = wide + cells * other

    def send(src, dst, k):
        return pltpu.make_async_remote_copy(
            src_ref=src, dst_ref=dst, send_sem=ssem.at[k], recv_sem=rsem.at[k],
            device_id=peer, device_id_type=pl.DeviceIdType.MESH,
        )

    def tap_copy(t):
        return pltpu.make_async_copy(kern.at[t], kbuf.at[t, pl.ds(0, width)], ksem.at[t])

    act_copy = pltpu.make_async_copy(act, field.at[rows(mine, cells)], lsem.at[0])
    df_copy = pltpu.make_async_copy(df, kbuf.at[:, ranks], lsem.at[1])
    act_copy.start()
    df_copy.start()
    for t in range(9):
        tap_copy(t).start()
    cot_copies = []
    for h in range(2):
        cot_copies.append(
            pltpu.make_async_copy(
                cot.at[:, pl.ds(h * width, width)], cotv.at[h], lsem.at[2 + h]
            )
        )
        cot_copies[-1].start()

    barrier = pltpu.get_barrier_semaphore()
    pl.semaphore_signal(barrier, inc=1, device_id=peer, device_id_type=pl.DeviceIdType.MESH)
    pl.semaphore_wait(barrier, 1)

    far = cells - chunk - wide
    spans = (
        ((cells - wide) * other, wide),
        (far * other + wide * y, chunk),
        ((wide + chunk) * y, far),
    )
    df_send = send(df, kbuf.at[:, ranks], 0)
    df_send.start()
    moves = [
        send(act.at[rows(start, size)], field.at[rows(mine + start, size)], 1 + n)
        for n, (start, size) in enumerate(spans)
    ]
    for move in moves:
        move.start()

    field[pl.ds(0, wide), :] = jnp.zeros((wide, channels), BF16)
    field[pl.ds(wide + total, wide), :] = jnp.zeros((wide, channels), BF16)
    act_copy.wait()
    df_copy.wait()
    df_send.wait_recv()
    moves[0].wait_recv()

    def conv(first_cell, count, low, first):
        part[:, pl.ds(0, count), :] = jnp.zeros((3, count, part.shape[2]), F32)

        def tap(t, carry):
            if first:
                tap_copy(t).wait()
            shifted = field[rows(first_cell + wide * (t // 3), count), :]
            part[t % 3, pl.ds(0, count), :] += lax.dot_general(
                shifted, kbuf[t], NT, preferred_element_type=F32
            )
            return carry

        lax.fori_loop(0, 9, tap, 0)

        def join(r, carry):
            span = rows(r * wide, wide)
            col = lax.broadcasted_iota(jnp.int32, (wide, part.shape[2]), 0)
            whole = (
                part[1, span, :]
                + jnp.where(col > 0, pltpu.roll(part[0, span, :], 1, 0), 0.0)
                + jnp.where(col < wide - 1, pltpu.roll(part[2, span, :], wide - 1, 0), 0.0)
            )
            bbuf[span, :] = whole[:, :width].astype(BF16)
            low[span, :] = whole[:, width:].astype(BF16)
            return carry

        lax.fori_loop(0, count // wide, join, 0)

    def finish(count, low):
        return (
            bbuf[pl.ds(0, count), :].astype(F32)
            + jnp.dot(low[pl.ds(0, count), :], up[y], preferred_element_type=F32)
        ).astype(BF16)

    conv(cells * y, cells, lown, True)
    block[y] = finish(cells, lown)

    moves[1].wait_recv()
    near = chunk * y
    conv(cells * other + near, chunk, lowp, False)
    ysend[rows(near, chunk), :] = finish(chunk, lowp)
    near_send = send(ysend.at[rows(near, chunk)], block.at[y, rows(near, chunk)], 4)
    near_send.start()

    moves[2].wait_recv()
    rest = chunk * other
    conv(cells * other + rest, chunk, lowp, False)
    ysend[rows(rest, chunk), :] = finish(chunk, lowp)
    rest_send = send(ysend.at[rows(rest, chunk)], block.at[y, rows(rest, chunk)], 5)
    rest_send.start()

    for copy in cot_copies:
        copy.wait()
    weight = wgt[0]

    def slopes(h, start, count):
        def step(r, carry):
            span = rows(start + r * wide, wide)
            value = block[h, span, :].astype(F32)
            sigma = jax.nn.sigmoid(value)
            slope[h, span, :] = (
                cotv[h, span, :].astype(F32) * weight * sigma * (1.0 + value * (1.0 - sigma))
            ).astype(BF16)
            return carry

        lax.fori_loop(0, count // wide, step, 0)

    slopes(y, 0, cells)
    near_send.wait_recv()
    slopes(other, chunk * other, chunk)
    rest_send.wait_recv()
    outs = [
        pltpu.make_async_copy(block.at[h], out.at[:, pl.ds(h * width, width)], lsem.at[4 + h])
        for h in range(2)
    ]
    for copy in outs:
        copy.start()
    slopes(other, chunk * y, chunk)

    grad = lax.dot_general(up[0], slope[0], NT, preferred_element_type=F32) + lax.dot_general(
        up[1], slope[1], NT, preferred_element_type=F32
    )
    lgt[...] = grad.astype(BF16)
    lanes = pl.ds(pl.multiple_of(cells * y, 128), cells)
    lg_send = send(lgt.at[pl.ds(pl.multiple_of(half * other, half), half)], lgall.at[:, lanes], 6)
    lg_send.start()
    for h in range(2):
        upp[h] = lax.dot_general(lown[...], slope[h], TN, preferred_element_type=F32)
    up_send = send(upp, upr, 7)
    up_send.start()
    lgall[:, lanes] = lgt[pl.ds(pl.multiple_of(half * y, half), half), :]
    lg_send.wait_recv()

    grads = lgall[...].astype(F32)
    place = lax.broadcasted_iota(jnp.int32, (half, total), 1)
    row, col = place // wide, place % wide
    high = total // wide
    for t in range(9):
        da, db = t // 3 - 1, t % 3 - 1
        offset = (da * wide + db) % total
        moved = pltpu.roll(grads, offset, 1) if offset else grads
        inside = (row >= da) & (row < high + da) & (col >= db) & (col < wide + db)
        taps[pl.ds(t * half, half), :] = jnp.where(inside, moved, 0.0).astype(BF16)
    down_out[...] = jnp.dot(
        taps[...], field[pl.ds(wide, total), :], preferred_element_type=F32
    ).astype(BF16)
    up_send.wait_recv()
    for h in range(2):
        up_out[:, pl.ds(h * width, width)] = (upp[h] + upr[h]).astype(BF16)
    for copy in [df_send, *moves, near_send, rest_send, lg_send, up_send]:
        copy.wait_send()
    for copy in outs:
        copy.wait()


def local_pair(
    activations, cotangent, base_kernel, down_table, up_table, sample_tenant, tenant_slot, timesteps
):
    width = base_kernel.shape[1]
    _, height, wide, channels = activations.shape
    cells = height * wide
    chunk = cells // 2
    tenants, _, _, half, block_cols = down_table.shape
    rank = up_table.shape[1]
    kernel_taps = jnp.transpose(base_kernel, (0, 2, 1, 3)).reshape(9, width, channels)
    all_tenants = lax.all_gather(sample_tenant, "ten", axis=0, tiled=True)
    all_slots = tenant_slot[all_tenants]
    groups = all_slots.shape[0]
    picks = (all_slots[:, None] == jnp.arange(tenants, dtype=jnp.int32)[None, :]).astype(BF16)
    table = jnp.concatenate([down_table.reshape(tenants, 9 * half, block_cols), up_table], axis=1)
    sent = jnp.einsum("dl,lkc->dkc", picks, table, preferred_element_type=F32).astype(BF16)
    factors = lax.all_to_all(sent, "ten", split_axis=0, concat_axis=0, tiled=True)
    factors = jnp.transpose(factors, (1, 0, 2)).reshape(9 * half + rank, channels)
    df = factors[: 9 * half].reshape(9, half, channels)
    up = jnp.transpose(factors[9 * half :].reshape(rank, 2, width), (1, 0, 2))
    weight = 1.0 / (1.0 + timesteps.astype(F32) / 250.0)

    anywhere = pl.BlockSpec(memory_space=pl.ANY)
    vmem = pl.BlockSpec(memory_space=pltpu.VMEM)
    block_out, down_term, up_term = pl.pallas_call(
        functools.partial(core_kernel, wide=wide, chunk=chunk),
        out_shape=(
            jax.ShapeDtypeStruct((cells, channels), BF16),
            jax.ShapeDtypeStruct((9 * half, channels), BF16),
            jax.ShapeDtypeStruct((rank, channels), BF16),
        ),
        in_specs=[anywhere] * 4 + [vmem, pl.BlockSpec(memory_space=pltpu.SMEM)],
        out_specs=(anywhere, vmem, vmem),
        scratch_shapes=[
            pltpu.VMEM((2 * cells + 2 * wide, channels), BF16),
            pltpu.VMEM((9, width + rank, channels), BF16),
            pltpu.VMEM((3, cells, width + rank), F32),
            pltpu.VMEM((cells, rank), BF16),
            pltpu.VMEM((chunk, rank), BF16),
            pltpu.VMEM((cells, width), BF16),
            pltpu.VMEM((2, cells, width), BF16),
            pltpu.VMEM((cells, width), BF16),
            pltpu.VMEM((2, cells, width), BF16),
            pltpu.VMEM((2, cells, width), BF16),
            pltpu.VMEM((rank, cells), BF16),
            pltpu.VMEM((half, 2 * cells), BF16),
            pltpu.VMEM((9 * half, 2 * cells), BF16),
            pltpu.VMEM((2, rank, width), F32),
            pltpu.VMEM((2, rank, width), F32),
            pltpu.SemaphoreType.DMA((9,)),
            pltpu.SemaphoreType.DMA((6,)),
            pltpu.SemaphoreType.DMA((8,)),
            pltpu.SemaphoreType.DMA((8,)),
        ],
        compiler_params=pltpu.CompilerParams(
            collective_id=0, has_side_effects=True, vmem_limit_bytes=56 * 1024 * 1024
        ),
    )(
        activations.reshape(cells, channels),
        cotangent.reshape(cells, channels),
        kernel_taps,
        df,
        up,
        weight,
    )
    terms = jnp.concatenate([down_term, up_term], axis=0).reshape(-1, groups, block_cols)
    terms = jnp.transpose(terms, (1, 0, 2))
    pieces = lax.all_to_all(terms, "ten", split_axis=0, concat_axis=0, tiled=True)
    sums = jnp.einsum("dl,dkc->lkc", picks, pieces, preferred_element_type=F32).astype(BF16)
    return (
        block_out.reshape(activations.shape),
        sums[:, : 9 * half].reshape(down_table.shape),
        sums[:, 9 * half :],
    )


def solution(mesh):
    placed = (
        P("ten", "fsdp", None, None),
        P("ten", "fsdp", None, None),
        P(None, "fsdp", None, None),
        P(None, None, None, "fsdp", "ten"),
        P(None, None, "ten"),
        P("ten"),
        P(),
        P("ten"),
    )
    return jax.shard_map(
        local_pair if mesh.shape["fsdp"] == 2 else local,
        mesh=mesh,
        in_specs=placed,
        out_specs=(
            P("ten", "fsdp", None, None),
            P(None, None, None, "fsdp", "ten"),
            P(None, None, "ten"),
        ),
        check_vma=False,
    )
```

```python
import functools

import jax
import jax.numpy as jnp
from jax import lax
from jax.experimental import pallas as pl
from jax.experimental.pallas import tpu as pltpu
from jax.sharding import PartitionSpec as P


def conv_same(field, kernel):
    return lax.conv_general_dilated(
        field,
        kernel,
        (1, 1),
        "SAME",
        dimension_numbers=("NHWC", "HWIO", "NHWC"),
        preferred_element_type=jnp.float32,
    )


def slope_of(block, cotangent, weight):
    value = block.astype(jnp.float32)
    sigma = jax.nn.sigmoid(value)
    return (cotangent.astype(jnp.float32) * weight * sigma * (1.0 + value * (1.0 - sigma))).astype(
        jnp.bfloat16
    )


def local(
    activations, cotangent, base_kernel, down_table, up_table, sample_tenant, tenant_slot, timesteps
):
    width = base_kernel.shape[1]
    kernel_hwio = jnp.transpose(base_kernel, (0, 2, 3, 1))
    ten_index = lax.axis_index("ten")
    fsdp_index = lax.axis_index("fsdp")
    tenants = down_table.shape[0]
    rank = up_table.shape[1]
    block_cols = down_table.shape[4]
    all_tenants = lax.all_gather(sample_tenant, "ten", axis=0, tiled=True)
    all_slots = tenant_slot[all_tenants]
    groups = all_slots.shape[0]
    picks = (all_slots[:, None] == jnp.arange(tenants, dtype=jnp.int32)[None, :]).astype(
        jnp.bfloat16
    )
    send_down = jnp.einsum(
        "dl,labkc->dabkc", picks, down_table, preferred_element_type=jnp.float32
    ).astype(jnp.bfloat16)
    send_up = jnp.einsum("dl,lkc->dkc", picks, up_table, preferred_element_type=jnp.float32).astype(
        jnp.bfloat16
    )
    send_up = send_up.reshape(groups, 1, 1, rank, block_cols)
    recv_down, recv_up = (
        lax.all_to_all(send_down, "ten", split_axis=0, concat_axis=4, tiled=True),
        lax.all_to_all(send_up, "ten", split_axis=0, concat_axis=4, tiled=True),
    )
    down_fac = recv_down[0]
    up_whole = recv_up[0, 0, 0]
    up_fac = lax.dynamic_slice_in_dim(up_whole, fsdp_index * width, width, 1)
    whole = lax.all_gather(activations, "fsdp", axis=1, tiled=True)
    height = whole.shape[1]
    breadth = whole.shape[2]
    cells = height * breadth
    base_part = conv_same(whole, kernel_hwio).astype(jnp.bfloat16)
    low_slice = conv_same(whole, jnp.transpose(down_fac, (0, 1, 3, 2))).astype(jnp.bfloat16)
    low = lax.all_gather(low_slice, "fsdp", axis=3, tiled=True).reshape(cells, rank)
    y_cols = (
        base_part.reshape(cells, width).astype(jnp.float32)
        + jnp.dot(low, up_fac, preferred_element_type=jnp.float32)
    ).astype(jnp.bfloat16)
    y_cols = y_cols.reshape(1, height, breadth, width)
    block_out = lax.all_to_all(y_cols, "fsdp", split_axis=1, concat_axis=3, tiled=True)
    weight = 1.0 / (1.0 + timesteps[0].astype(jnp.float32) / 250.0)
    slope = lax.all_to_all(
        slope_of(block_out, cotangent, weight), "fsdp", split_axis=3, concat_axis=1, tiled=True
    )
    slope = slope.reshape(cells, width)
    up_term = lax.dot_general(
        low, slope, (((0,), (0,)), ((), ())), preferred_element_type=jnp.float32
    ).astype(jnp.bfloat16)
    grad_part = lax.dot_general(
        slope, up_fac, (((1,), (1,)), ((), ())), preferred_element_type=jnp.float32
    )
    low_grad = lax.psum_scatter(grad_part, "fsdp", scatter_dimension=1, tiled=True).astype(
        jnp.bfloat16
    )
    padded = jnp.pad(whole[0], ((1, 1), (1, 1), (0, 0)))
    channels = whole.shape[3]
    rows_list = []
    for tap_row in range(3):
        cols_list = []
        for tap_col in range(3):
            shifted = padded[tap_row : tap_row + height, tap_col : tap_col + breadth].reshape(
                cells, channels
            )
            cols_list.append(
                lax.dot_general(
                    low_grad, shifted, (((0,), (0,)), ((), ())), preferred_element_type=jnp.float32
                )
            )
        rows_list.append(jnp.stack(cols_list))
    down_term = jnp.stack(rows_list).astype(jnp.bfloat16)
    up_all = lax.all_gather(up_term, "fsdp", axis=1, tiled=True)
    down_piece = lax.all_to_all(down_term[None], "ten", split_axis=4, concat_axis=0, tiled=True)
    up_piece = lax.all_to_all(up_all[None], "ten", split_axis=2, concat_axis=0, tiled=True)
    down_sum = jnp.einsum("dl,dabkc->labkc", picks, down_piece, preferred_element_type=jnp.float32)
    up_sum = jnp.einsum("dl,dkc->lkc", picks, up_piece, preferred_element_type=jnp.float32)
    return (block_out, down_sum.astype(jnp.bfloat16), up_sum.astype(jnp.bfloat16))


NT = (((1,), (1,)), ((), ()))
TN = (((0,), (0,)), ((), ()))
F32 = jnp.float32
BF16 = jnp.bfloat16


def core_kernel(
    act, cot, kern, table, tenant, slot_of, wgt, out, pieces_out, slots_out,
    slot_mine, slots, slots_s, fac_send, fac_recv, fac, fin, fin_recv, up,
    field, kbuf, part, lown, lowp, bbuf, block, ysend, cotv, slope, lgt, lgall, taps, upp, upr,
    ksem, lsem, ssem, rsem, tsend, trecv, *, wide, chunk,
):
    me = lax.axis_index("ten")
    terms, block_cols = table.shape[1], table.shape[2]
    groups = slots.shape[0]
    y = lax.axis_index("fsdp")
    other = 1 - y
    peer = {"fsdp": other}
    cells, channels = act.shape
    width = kern.shape[1]
    half = lgall.shape[0]
    rank = 2 * half
    total = 2 * cells

    def rows(start, size):
        return pl.ds(pl.multiple_of(start, wide), size)

    ranks = pl.ds(pl.multiple_of(width + half * y, half), half)
    mine = wide + cells * y
    theirs = wide + cells * other

    def send(src, dst, k):
        return pltpu.make_async_remote_copy(
            src_ref=src, dst_ref=dst, send_sem=ssem.at[k], recv_sem=rsem.at[k],
            device_id=peer, device_id_type=pl.DeviceIdType.MESH,
        )

    def tap_copy(t):
        return pltpu.make_async_copy(kern.at[t], kbuf.at[t, pl.ds(0, width)], ksem.at[t])

    act_copy = pltpu.make_async_copy(act, field.at[rows(mine, cells)], lsem.at[0])
    act_copy.start()
    for t in range(9):
        tap_copy(t).start()
    cot_copies = []
    for h in range(2):
        cot_copies.append(
            pltpu.make_async_copy(
                cot.at[:, pl.ds(h * width, width)], cotv.at[h], lsem.at[2 + h]
            )
        )
        cot_copies[-1].start()

    def ten_copy(src, dst, kind, k, source):
        return pltpu.make_async_remote_copy(
            src_ref=src, dst_ref=dst, send_sem=tsend.at[kind, k], recv_sem=trecv.at[kind, source],
            device_id={"ten": lax.rem(me + k, groups)}, device_id_type=pl.DeviceIdType.MESH,
        )

    def each_other(body):
        def step(k, carry):
            body(k)
            return carry

        lax.fori_loop(1, groups, step, 0)

    def arrived(src, dst, kind):
        def body(k):
            source = lax.rem(me + k, groups)
            ten_copy(src.at[source], dst.at[source], kind, k, source).wait_recv()

        each_other(body)

    slot_mine[...] = jnp.full(slot_mine.shape, slot_of[tenant[0]], jnp.int32)
    slots[me] = slot_mine[0]
    barrier = pltpu.get_barrier_semaphore()
    pl.semaphore_signal(barrier, inc=1, device_id=peer, device_id_type=pl.DeviceIdType.MESH)

    def greet(k):
        pl.semaphore_signal(
            barrier, inc=1, device_id={"ten": lax.rem(me + k, groups)},
            device_id_type=pl.DeviceIdType.MESH,
        )

    each_other(greet)
    pl.semaphore_wait(barrier, groups)
    each_other(lambda k: ten_copy(slot_mine.at[0], slots.at[me], 0, k, me).start())

    far = cells - chunk - wide
    spans = (
        ((cells - wide) * other, wide),
        (far * other + wide * y, chunk),
        ((wide + chunk) * y, far),
    )
    moves = [
        send(act.at[rows(start, size)], field.at[rows(mine + start, size)], 1 + n)
        for n, (start, size) in enumerate(spans)
    ]
    for move in moves:
        move.start()

    field[pl.ds(0, wide), :] = jnp.zeros((wide, channels), BF16)
    field[pl.ds(wide + total, wide), :] = jnp.zeros((wide, channels), BF16)

    arrived(slots, slots, 0)
    slots_out[...] = slots[...]
    slot_copy = pltpu.make_async_copy(slots, slots_s, lsem.at[1])
    slot_copy.start()
    slot_copy.wait()

    def pick(d, carry):
        fac_send[d] = table[slots_s[d, 0, 0]]
        return carry

    lax.fori_loop(0, groups, pick, 0)
    fac_recv[me] = fac_send[me]
    each_other(
        lambda k: ten_copy(
            fac_send.at[lax.rem(me + k, groups)], fac_recv.at[me], 1, k, me
        ).start()
    )
    act_copy.wait()
    moves[0].wait_recv()

    def products(first_cell, count, columns, first):
        part[:, pl.ds(0, count), columns] = jnp.zeros((3, count, columns.size), F32)

        def tap(t, carry):
            if first:
                tap_copy(t).wait()
            shifted = field[rows(first_cell + wide * (t // 3), count), :]
            part[t % 3, pl.ds(0, count), columns] += lax.dot_general(
                shifted, kbuf[t, columns, :], NT, preferred_element_type=F32
            )
            return carry

        lax.fori_loop(0, 9, tap, 0)

    def joined(count, low):
        def join(r, carry):
            span = rows(r * wide, wide)
            col = lax.broadcasted_iota(jnp.int32, (wide, part.shape[2]), 0)
            whole = (
                part[1, span, :]
                + jnp.where(col > 0, pltpu.roll(part[0, span, :], 1, 0), 0.0)
                + jnp.where(col < wide - 1, pltpu.roll(part[2, span, :], wide - 1, 0), 0.0)
            )
            bbuf[span, :] = whole[:, :width].astype(BF16)
            low[span, :] = whole[:, width:].astype(BF16)
            return carry

        lax.fori_loop(0, count // wide, join, 0)

    def finish(count, low):
        return (
            bbuf[pl.ds(0, count), :].astype(F32)
            + jnp.dot(low[pl.ds(0, count), :], up[y], preferred_element_type=F32)
        ).astype(BF16)

    products(cells * y, cells, pl.ds(0, width), True)

    arrived(fac_send, fac_recv, 1)
    for first in range(0, groups, 8):
        span = pl.ds(first * block_cols, 8 * block_cols)
        fac[:, span] = jnp.concatenate(
            [fac_recv[d].astype(F32) for d in range(first, first + 8)], axis=1
        ).astype(BF16)
    for t in range(9):
        kbuf[t, ranks, :] = fac[pl.ds(t * half, half), :]
    for h in range(2):
        up[h] = fac[pl.ds(9 * half, rank), pl.ds(h * width, width)]
    df_send = send(kbuf.at[:, ranks], kbuf.at[:, ranks], 0)
    df_send.start()
    df_send.wait_recv()
    products(cells * y, cells, pl.ds(width, rank), False)
    joined(cells, lown)
    block[y] = finish(cells, lown)

    moves[1].wait_recv()
    near = chunk * y
    products(cells * other + near, chunk, pl.ds(0, width + rank), False)
    joined(chunk, lowp)
    ysend[rows(near, chunk), :] = finish(chunk, lowp)
    near_send = send(ysend.at[rows(near, chunk)], block.at[y, rows(near, chunk)], 4)
    near_send.start()

    moves[2].wait_recv()
    rest = chunk * other
    products(cells * other + rest, chunk, pl.ds(0, width + rank), False)
    joined(chunk, lowp)
    ysend[rows(rest, chunk), :] = finish(chunk, lowp)
    rest_send = send(ysend.at[rows(rest, chunk)], block.at[y, rows(rest, chunk)], 5)
    rest_send.start()

    for copy in cot_copies:
        copy.wait()
    weight = wgt[0]

    def slopes(h, start, count):
        def step(r, carry):
            span = rows(start + r * wide, wide)
            value = block[h, span, :].astype(F32)
            sigma = jax.nn.sigmoid(value)
            slope[h, span, :] = (
                cotv[h, span, :].astype(F32) * weight * sigma * (1.0 + value * (1.0 - sigma))
            ).astype(BF16)
            return carry

        lax.fori_loop(0, count // wide, step, 0)

    slopes(y, 0, cells)
    near_send.wait_recv()
    slopes(other, chunk * other, chunk)
    rest_send.wait_recv()
    outs = [
        pltpu.make_async_copy(block.at[h], out.at[:, pl.ds(h * width, width)], lsem.at[4 + h])
        for h in range(2)
    ]
    for copy in outs:
        copy.start()
    slopes(other, chunk * y, chunk)

    grad = lax.dot_general(up[0], slope[0], NT, preferred_element_type=F32) + lax.dot_general(
        up[1], slope[1], NT, preferred_element_type=F32
    )
    lgt[...] = grad.astype(BF16)
    lanes = pl.ds(pl.multiple_of(cells * y, 128), cells)
    lg_send = send(lgt.at[pl.ds(pl.multiple_of(half * other, half), half)], lgall.at[:, lanes], 6)
    lg_send.start()
    for h in range(2):
        upp[h] = lax.dot_general(lown[...], slope[h], TN, preferred_element_type=F32)
    up_send = send(upp, upr, 7)
    up_send.start()
    lgall[:, lanes] = lgt[pl.ds(pl.multiple_of(half * y, half), half), :]
    lg_send.wait_recv()

    grads = lgall[...].astype(F32)
    place = lax.broadcasted_iota(jnp.int32, (half, total), 1)
    row, col = place // wide, place % wide
    high = total // wide
    for t in range(9):
        da, db = t // 3 - 1, t % 3 - 1
        offset = (da * wide + db) % total
        moved = pltpu.roll(grads, offset, 1) if offset else grads
        inside = (row >= da) & (row < high + da) & (col >= db) & (col < wide + db)
        taps[pl.ds(t * half, half), :] = jnp.where(inside, moved, 0.0).astype(BF16)
    each_other(
        lambda k: ten_copy(
            fac_send.at[lax.rem(me + k, groups)], fac_recv.at[me], 1, k, me
        ).wait_send()
    )
    fin[pl.ds(0, 9 * half), :] = jnp.dot(
        taps[...], field[pl.ds(wide, total), :], preferred_element_type=F32
    )
    up_send.wait_recv()
    for h in range(2):
        fin[pl.ds(9 * half, rank), pl.ds(h * width, width)] = upp[h] + upr[h]
    for d in range(groups):
        fac_send[d] = fin[:, pl.ds(d * block_cols, block_cols)].astype(BF16)
    each_other(
        lambda k: ten_copy(
            fac_send.at[lax.rem(me + k, groups)], fin_recv.at[me], 2, k, me
        ).start()
    )
    fin_recv[me] = fac_send[me]
    arrived(fac_send, fin_recv, 2)
    pieces_out[...] = fin_recv[...]
    each_other(lambda k: ten_copy(slot_mine.at[0], slots.at[me], 0, k, me).wait_send())
    each_other(
        lambda k: ten_copy(
            fac_send.at[lax.rem(me + k, groups)], fin_recv.at[me], 2, k, me
        ).wait_send()
    )
    for copy in [df_send, *moves, near_send, rest_send, lg_send, up_send]:
        copy.wait_send()
    for copy in outs:
        copy.wait()


def local_pair(
    activations, cotangent, base_kernel, down_table, up_table, sample_tenant, tenant_slot, timesteps
):
    width = base_kernel.shape[1]
    _, height, wide, channels = activations.shape
    cells = height * wide
    chunk = cells // 2
    tenants, _, _, half, block_cols = down_table.shape
    rank = up_table.shape[1]
    kernel_taps = jnp.transpose(base_kernel, (0, 2, 1, 3)).reshape(9, width, channels)
    groups = lax.axis_size("ten")
    terms = 9 * half + rank
    table = jnp.concatenate([down_table.reshape(tenants, 9 * half, block_cols), up_table], axis=1)
    weight = 1.0 / (1.0 + timesteps.astype(F32) / 250.0)

    anywhere = pl.BlockSpec(memory_space=pl.ANY)
    vmem = pl.BlockSpec(memory_space=pltpu.VMEM)
    block_out, pieces, slots = pl.pallas_call(
        functools.partial(core_kernel, wide=wide, chunk=chunk),
        out_shape=(
            jax.ShapeDtypeStruct((cells, channels), BF16),
            jax.ShapeDtypeStruct((groups, terms, block_cols), BF16),
            jax.ShapeDtypeStruct((groups, 1, 128), jnp.int32),
        ),
        in_specs=[anywhere] * 3 + [vmem] + [pl.BlockSpec(memory_space=pltpu.SMEM)] * 3,
        out_specs=(anywhere, vmem, vmem),
        scratch_shapes=[
            pltpu.VMEM((1, 1, 128), jnp.int32),
            pltpu.VMEM((groups, 1, 128), jnp.int32),
            pltpu.SMEM((groups, 1, 128), jnp.int32),
            pltpu.VMEM((groups, terms, block_cols), BF16),
            pltpu.VMEM((groups, terms, block_cols), BF16),
            pltpu.VMEM((terms, channels), BF16),
            pltpu.VMEM((terms, channels), F32),
            pltpu.VMEM((groups, terms, block_cols), BF16),
            pltpu.VMEM((2, rank, width), BF16),
            pltpu.VMEM((2 * cells + 2 * wide, channels), BF16),
            pltpu.VMEM((9, width + rank, channels), BF16),
            pltpu.VMEM((3, cells, width + rank), F32),
            pltpu.VMEM((cells, rank), BF16),
            pltpu.VMEM((chunk, rank), BF16),
            pltpu.VMEM((cells, width), BF16),
            pltpu.VMEM((2, cells, width), BF16),
            pltpu.VMEM((cells, width), BF16),
            pltpu.VMEM((2, cells, width), BF16),
            pltpu.VMEM((2, cells, width), BF16),
            pltpu.VMEM((rank, cells), BF16),
            pltpu.VMEM((half, 2 * cells), BF16),
            pltpu.VMEM((9 * half, 2 * cells), BF16),
            pltpu.VMEM((2, rank, width), F32),
            pltpu.VMEM((2, rank, width), F32),
            pltpu.SemaphoreType.DMA((9,)),
            pltpu.SemaphoreType.DMA((6,)),
            pltpu.SemaphoreType.DMA((8,)),
            pltpu.SemaphoreType.DMA((8,)),
            pltpu.SemaphoreType.DMA((3, groups)),
            pltpu.SemaphoreType.DMA((3, groups)),
        ],
        compiler_params=pltpu.CompilerParams(
            collective_id=0, has_side_effects=True, vmem_limit_bytes=56 * 1024 * 1024
        ),
    )(
        activations.reshape(cells, channels),
        cotangent.reshape(cells, channels),
        kernel_taps,
        table,
        sample_tenant,
        tenant_slot,
        weight,
    )
    picks = (slots[:, 0, :1] == jnp.arange(tenants, dtype=jnp.int32)[None, :]).astype(BF16)
    sums = jnp.einsum("dl,dkc->lkc", picks, pieces, preferred_element_type=F32).astype(BF16)
    return (
        block_out.reshape(activations.shape),
        sums[:, : 9 * half].reshape(down_table.shape),
        sums[:, 9 * half :],
    )


def solution(mesh):
    placed = (
        P("ten", "fsdp", None, None),
        P("ten", "fsdp", None, None),
        P(None, "fsdp", None, None),
        P(None, None, None, "fsdp", "ten"),
        P(None, None, "ten"),
        P("ten"),
        P(),
        P("ten"),
    )
    return jax.shard_map(
        local_pair if mesh.shape["fsdp"] == 2 else local,
        mesh=mesh,
        in_specs=placed,
        out_specs=(
            P("ten", "fsdp", None, None),
            P(None, None, None, "fsdp", "ten"),
            P(None, None, "ten"),
        ),
        check_vma=False,
    )
```

```python
import functools

import jax
import jax.numpy as jnp
from jax import lax
from jax.experimental import pallas as pl
from jax.experimental.pallas import tpu as pltpu
from jax.sharding import PartitionSpec as P


def conv_same(field, kernel):
    return lax.conv_general_dilated(
        field,
        kernel,
        (1, 1),
        "SAME",
        dimension_numbers=("NHWC", "HWIO", "NHWC"),
        preferred_element_type=jnp.float32,
    )


def slope_of(block, cotangent, weight):
    value = block.astype(jnp.float32)
    sigma = jax.nn.sigmoid(value)
    return (cotangent.astype(jnp.float32) * weight * sigma * (1.0 + value * (1.0 - sigma))).astype(
        jnp.bfloat16
    )


def local(
    activations, cotangent, base_kernel, down_table, up_table, sample_tenant, tenant_slot, timesteps
):
    width = base_kernel.shape[1]
    kernel_hwio = jnp.transpose(base_kernel, (0, 2, 3, 1))
    ten_index = lax.axis_index("ten")
    fsdp_index = lax.axis_index("fsdp")
    tenants = down_table.shape[0]
    rank = up_table.shape[1]
    block_cols = down_table.shape[4]
    all_tenants = lax.all_gather(sample_tenant, "ten", axis=0, tiled=True)
    all_slots = tenant_slot[all_tenants]
    groups = all_slots.shape[0]
    picks = (all_slots[:, None] == jnp.arange(tenants, dtype=jnp.int32)[None, :]).astype(
        jnp.bfloat16
    )
    send_down = jnp.einsum(
        "dl,labkc->dabkc", picks, down_table, preferred_element_type=jnp.float32
    ).astype(jnp.bfloat16)
    send_up = jnp.einsum("dl,lkc->dkc", picks, up_table, preferred_element_type=jnp.float32).astype(
        jnp.bfloat16
    )
    send_up = send_up.reshape(groups, 1, 1, rank, block_cols)
    recv_down, recv_up = (
        lax.all_to_all(send_down, "ten", split_axis=0, concat_axis=4, tiled=True),
        lax.all_to_all(send_up, "ten", split_axis=0, concat_axis=4, tiled=True),
    )
    down_fac = recv_down[0]
    up_whole = recv_up[0, 0, 0]
    up_fac = lax.dynamic_slice_in_dim(up_whole, fsdp_index * width, width, 1)
    whole = lax.all_gather(activations, "fsdp", axis=1, tiled=True)
    height = whole.shape[1]
    breadth = whole.shape[2]
    cells = height * breadth
    base_part = conv_same(whole, kernel_hwio).astype(jnp.bfloat16)
    low_slice = conv_same(whole, jnp.transpose(down_fac, (0, 1, 3, 2))).astype(jnp.bfloat16)
    low = lax.all_gather(low_slice, "fsdp", axis=3, tiled=True).reshape(cells, rank)
    y_cols = (
        base_part.reshape(cells, width).astype(jnp.float32)
        + jnp.dot(low, up_fac, preferred_element_type=jnp.float32)
    ).astype(jnp.bfloat16)
    y_cols = y_cols.reshape(1, height, breadth, width)
    block_out = lax.all_to_all(y_cols, "fsdp", split_axis=1, concat_axis=3, tiled=True)
    weight = 1.0 / (1.0 + timesteps[0].astype(jnp.float32) / 250.0)
    slope = lax.all_to_all(
        slope_of(block_out, cotangent, weight), "fsdp", split_axis=3, concat_axis=1, tiled=True
    )
    slope = slope.reshape(cells, width)
    up_term = lax.dot_general(
        low, slope, (((0,), (0,)), ((), ())), preferred_element_type=jnp.float32
    ).astype(jnp.bfloat16)
    grad_part = lax.dot_general(
        slope, up_fac, (((1,), (1,)), ((), ())), preferred_element_type=jnp.float32
    )
    low_grad = lax.psum_scatter(grad_part, "fsdp", scatter_dimension=1, tiled=True).astype(
        jnp.bfloat16
    )
    padded = jnp.pad(whole[0], ((1, 1), (1, 1), (0, 0)))
    channels = whole.shape[3]
    rows_list = []
    for tap_row in range(3):
        cols_list = []
        for tap_col in range(3):
            shifted = padded[tap_row : tap_row + height, tap_col : tap_col + breadth].reshape(
                cells, channels
            )
            cols_list.append(
                lax.dot_general(
                    low_grad, shifted, (((0,), (0,)), ((), ())), preferred_element_type=jnp.float32
                )
            )
        rows_list.append(jnp.stack(cols_list))
    down_term = jnp.stack(rows_list).astype(jnp.bfloat16)
    up_all = lax.all_gather(up_term, "fsdp", axis=1, tiled=True)
    down_piece = lax.all_to_all(down_term[None], "ten", split_axis=4, concat_axis=0, tiled=True)
    up_piece = lax.all_to_all(up_all[None], "ten", split_axis=2, concat_axis=0, tiled=True)
    down_sum = jnp.einsum("dl,dabkc->labkc", picks, down_piece, preferred_element_type=jnp.float32)
    up_sum = jnp.einsum("dl,dkc->lkc", picks, up_piece, preferred_element_type=jnp.float32)
    return (block_out, down_sum.astype(jnp.bfloat16), up_sum.astype(jnp.bfloat16))


NT = (((1,), (1,)), ((), ()))
TN = (((0,), (0,)), ((), ()))
F32 = jnp.float32
BF16 = jnp.bfloat16


def core_kernel(
    act, cot, kern, table, tenant, slot_of, wgt, out, pieces_out, slots_out,
    slot_mine, slots, slots_s, fac_send, fac_recv, fac, fin, fin_recv, up,
    field, kbuf, part, lown, lowp, bbuf, block, ysend, cotv, slope, lgt, lgall, taps, upp, upr,
    ksem, lsem, ssem, rsem, tsend, trecv, *, wide, chunk,
):
    me = lax.axis_index("ten")
    terms, block_cols = table.shape[1], table.shape[2]
    groups = slots.shape[0]
    y = lax.axis_index("fsdp")
    other = 1 - y
    peer = {"fsdp": other}
    cells, channels = act.shape
    width = kern.shape[1]
    half = lgall.shape[0]
    rank = 2 * half
    total = 2 * cells

    def rows(start, size):
        return pl.ds(pl.multiple_of(start, wide), size)

    ranks = pl.ds(pl.multiple_of(width + half * y, half), half)
    mine = wide + cells * y
    theirs = wide + cells * other

    def send(src, dst, k):
        return pltpu.make_async_remote_copy(
            src_ref=src, dst_ref=dst, send_sem=ssem.at[k], recv_sem=rsem.at[k],
            device_id=peer, device_id_type=pl.DeviceIdType.MESH,
        )

    def tap_copy(t):
        return pltpu.make_async_copy(kern.at[t], kbuf.at[t, pl.ds(0, width)], ksem.at[t])

    act_copy = pltpu.make_async_copy(act, field.at[rows(mine, cells)], lsem.at[0])
    act_copy.start()
    for t in range(9):
        tap_copy(t).start()
    cot_copies = []
    for h in range(2):
        cot_copies.append(
            pltpu.make_async_copy(
                cot.at[:, pl.ds(h * width, width)], cotv.at[h], lsem.at[2 + h]
            )
        )
        cot_copies[-1].start()

    def ten_copy(src, dst, kind, k, source):
        return pltpu.make_async_remote_copy(
            src_ref=src, dst_ref=dst, send_sem=tsend.at[kind, k], recv_sem=trecv.at[kind, source],
            device_id={"ten": lax.rem(me + k, groups)}, device_id_type=pl.DeviceIdType.MESH,
        )

    def each_other(body):
        def step(k, carry):
            body(k)
            return carry

        lax.fori_loop(1, groups, step, 0)

    def arrived(src, dst, kind):
        def body(k):
            source = lax.rem(me + k, groups)
            ten_copy(src.at[source], dst.at[source], kind, k, source).wait_recv()

        each_other(body)

    slot_mine[...] = jnp.full(slot_mine.shape, slot_of[tenant[0]], jnp.int32)
    slots[me] = slot_mine[0]
    barrier = pltpu.get_barrier_semaphore()
    pl.semaphore_signal(barrier, inc=1, device_id=peer, device_id_type=pl.DeviceIdType.MESH)

    def greet(k):
        pl.semaphore_signal(
            barrier, inc=1, device_id={"ten": lax.rem(me + k, groups)},
            device_id_type=pl.DeviceIdType.MESH,
        )

    each_other(greet)
    pl.semaphore_wait(barrier, groups)
    each_other(lambda k: ten_copy(slot_mine.at[0], slots.at[me], 0, k, me).start())

    far = cells - chunk - wide
    spans = (
        ((cells - wide) * other, wide),
        (far * other + wide * y, chunk),
        ((wide + chunk) * y, far),
    )
    moves = [
        send(act.at[rows(start, size)], field.at[rows(mine + start, size)], 1 + n)
        for n, (start, size) in enumerate(spans)
    ]
    for move in moves:
        move.start()

    field[pl.ds(0, wide), :] = jnp.zeros((wide, channels), BF16)
    field[pl.ds(wide + total, wide), :] = jnp.zeros((wide, channels), BF16)

    arrived(slots, slots, 0)
    slots_out[...] = slots[...]
    slot_copy = pltpu.make_async_copy(slots, slots_s, lsem.at[1])
    slot_copy.start()
    slot_copy.wait()

    def pick(d, carry):
        fac_send[d] = table[slots_s[d, 0, 0]]
        return carry

    lax.fori_loop(0, groups, pick, 0)
    fac_recv[me] = fac_send[me]
    each_other(
        lambda k: ten_copy(
            fac_send.at[lax.rem(me + k, groups)], fac_recv.at[me], 1, k, me
        ).start()
    )
    act_copy.wait()
    moves[0].wait_recv()

    def products(first_cell, at, count, columns, first):
        part[:, pl.ds(at, count), columns] = jnp.zeros((3, count, columns.size), F32)

        def tap(t, carry):
            if first:
                tap_copy(t).wait()
            shifted = field[rows(first_cell + wide * (t // 3), count), :]
            part[t % 3, pl.ds(at, count), columns] += lax.dot_general(
                shifted, kbuf[t, columns, :], NT, preferred_element_type=F32
            )
            return carry

        lax.fori_loop(0, 9, tap, 0)

    def joined(at, count, low):
        def join(r, carry):
            span = rows(r * wide, wide)
            col = lax.broadcasted_iota(jnp.int32, (wide, part.shape[2]), 0)
            held = rows(at + r * wide, wide)
            whole = (
                part[1, held, :]
                + jnp.where(col > 0, pltpu.roll(part[0, held, :], 1, 0), 0.0)
                + jnp.where(col < wide - 1, pltpu.roll(part[2, held, :], wide - 1, 0), 0.0)
            )
            bbuf[span, :] = whole[:, :width].astype(BF16)
            low[span, :] = whole[:, width:].astype(BF16)
            return carry

        lax.fori_loop(0, count // wide, join, 0)

    def finish(count, low):
        return (
            bbuf[pl.ds(0, count), :].astype(F32)
            + jnp.dot(low[pl.ds(0, count), :], up[y], preferred_element_type=F32)
        ).astype(BF16)

    base, lows = pl.ds(0, width), pl.ds(width, rank)
    products(cells * y, 0, cells, base, True)

    arrived(fac_send, fac_recv, 1)
    for first in range(0, groups, 8):
        span = pl.ds(first * block_cols, 8 * block_cols)
        fac[:, span] = jnp.concatenate(
            [fac_recv[d].astype(F32) for d in range(first, first + 8)], axis=1
        ).astype(BF16)
    for t in range(9):
        kbuf[t, ranks, :] = fac[pl.ds(t * half, half), :]
    for h in range(2):
        up[h] = fac[pl.ds(9 * half, rank), pl.ds(h * width, width)]
    df_send = send(kbuf.at[:, ranks], kbuf.at[:, ranks], 0)
    df_send.start()
    near, rest = chunk * y, chunk * other
    moves[1].wait_recv()
    products(cells * other + near, cells, chunk, base, False)
    moves[2].wait_recv()
    products(cells * other + rest, cells + chunk, chunk, base, False)
    df_send.wait_recv()

    products(cells * other + near, cells, chunk, lows, False)
    joined(cells, chunk, lowp)
    ysend[rows(near, chunk), :] = finish(chunk, lowp)
    near_send = send(ysend.at[rows(near, chunk)], block.at[y, rows(near, chunk)], 4)
    near_send.start()

    products(cells * other + rest, cells + chunk, chunk, lows, False)
    joined(cells + chunk, chunk, lowp)
    ysend[rows(rest, chunk), :] = finish(chunk, lowp)
    rest_send = send(ysend.at[rows(rest, chunk)], block.at[y, rows(rest, chunk)], 5)
    rest_send.start()

    products(cells * y, 0, cells, lows, False)
    joined(0, cells, lown)
    block[y] = finish(cells, lown)

    for copy in cot_copies:
        copy.wait()
    weight = wgt[0]

    def slopes(h, start, count):
        def step(r, carry):
            span = rows(start + r * wide, wide)
            value = block[h, span, :].astype(F32)
            sigma = jax.nn.sigmoid(value)
            slope[h, span, :] = (
                cotv[h, span, :].astype(F32) * weight * sigma * (1.0 + value * (1.0 - sigma))
            ).astype(BF16)
            return carry

        lax.fori_loop(0, count // wide, step, 0)

    slopes(y, 0, cells)
    near_send.wait_recv()
    slopes(other, chunk * other, chunk)
    rest_send.wait_recv()
    outs = [
        pltpu.make_async_copy(block.at[h], out.at[:, pl.ds(h * width, width)], lsem.at[4 + h])
        for h in range(2)
    ]
    for copy in outs:
        copy.start()
    slopes(other, chunk * y, chunk)

    grad = lax.dot_general(up[0], slope[0], NT, preferred_element_type=F32) + lax.dot_general(
        up[1], slope[1], NT, preferred_element_type=F32
    )
    lgt[...] = grad.astype(BF16)
    lanes = pl.ds(pl.multiple_of(cells * y, 128), cells)
    lg_send = send(lgt.at[pl.ds(pl.multiple_of(half * other, half), half)], lgall.at[:, lanes], 6)
    lg_send.start()
    for h in range(2):
        upp[h] = lax.dot_general(lown[...], slope[h], TN, preferred_element_type=F32)
    up_send = send(upp, upr, 7)
    up_send.start()
    lgall[:, lanes] = lgt[pl.ds(pl.multiple_of(half * y, half), half), :]
    lg_send.wait_recv()

    grads = lgall[...].astype(F32)
    place = lax.broadcasted_iota(jnp.int32, (half, total), 1)
    row, col = place // wide, place % wide
    high = total // wide
    for t in range(9):
        da, db = t // 3 - 1, t % 3 - 1
        offset = (da * wide + db) % total
        moved = pltpu.roll(grads, offset, 1) if offset else grads
        inside = (row >= da) & (row < high + da) & (col >= db) & (col < wide + db)
        taps[pl.ds(t * half, half), :] = jnp.where(inside, moved, 0.0).astype(BF16)
    each_other(
        lambda k: ten_copy(
            fac_send.at[lax.rem(me + k, groups)], fac_recv.at[me], 1, k, me
        ).wait_send()
    )
    fin[pl.ds(0, 9 * half), :] = jnp.dot(
        taps[...], field[pl.ds(wide, total), :], preferred_element_type=F32
    )
    up_send.wait_recv()
    for h in range(2):
        fin[pl.ds(9 * half, rank), pl.ds(h * width, width)] = upp[h] + upr[h]
    for d in range(groups):
        fac_send[d] = fin[:, pl.ds(d * block_cols, block_cols)].astype(BF16)
    each_other(
        lambda k: ten_copy(
            fac_send.at[lax.rem(me + k, groups)], fin_recv.at[me], 2, k, me
        ).start()
    )
    fin_recv[me] = fac_send[me]
    arrived(fac_send, fin_recv, 2)
    pieces_out[...] = fin_recv[...]
    each_other(lambda k: ten_copy(slot_mine.at[0], slots.at[me], 0, k, me).wait_send())
    each_other(
        lambda k: ten_copy(
            fac_send.at[lax.rem(me + k, groups)], fin_recv.at[me], 2, k, me
        ).wait_send()
    )
    for copy in [df_send, *moves, near_send, rest_send, lg_send, up_send]:
        copy.wait_send()
    for copy in outs:
        copy.wait()


def local_pair(
    activations, cotangent, base_kernel, down_table, up_table, sample_tenant, tenant_slot, timesteps
):
    width = base_kernel.shape[1]
    _, height, wide, channels = activations.shape
    cells = height * wide
    chunk = cells // 2
    tenants, _, _, half, block_cols = down_table.shape
    rank = up_table.shape[1]
    kernel_taps = jnp.transpose(base_kernel, (0, 2, 1, 3)).reshape(9, width, channels)
    groups = lax.axis_size("ten")
    terms = 9 * half + rank
    table = jnp.concatenate([down_table.reshape(tenants, 9 * half, block_cols), up_table], axis=1)
    weight = 1.0 / (1.0 + timesteps.astype(F32) / 250.0)

    anywhere = pl.BlockSpec(memory_space=pl.ANY)
    vmem = pl.BlockSpec(memory_space=pltpu.VMEM)
    block_out, pieces, slots = pl.pallas_call(
        functools.partial(core_kernel, wide=wide, chunk=chunk),
        out_shape=(
            jax.ShapeDtypeStruct((cells, channels), BF16),
            jax.ShapeDtypeStruct((groups, terms, block_cols), BF16),
            jax.ShapeDtypeStruct((groups, 1, 128), jnp.int32),
        ),
        in_specs=[anywhere] * 3 + [vmem] + [pl.BlockSpec(memory_space=pltpu.SMEM)] * 3,
        out_specs=(anywhere, vmem, vmem),
        scratch_shapes=[
            pltpu.VMEM((1, 1, 128), jnp.int32),
            pltpu.VMEM((groups, 1, 128), jnp.int32),
            pltpu.SMEM((groups, 1, 128), jnp.int32),
            pltpu.VMEM((groups, terms, block_cols), BF16),
            pltpu.VMEM((groups, terms, block_cols), BF16),
            pltpu.VMEM((terms, channels), BF16),
            pltpu.VMEM((terms, channels), F32),
            pltpu.VMEM((groups, terms, block_cols), BF16),
            pltpu.VMEM((2, rank, width), BF16),
            pltpu.VMEM((2 * cells + 2 * wide, channels), BF16),
            pltpu.VMEM((9, width + rank, channels), BF16),
            pltpu.VMEM((3, 2 * cells, width + rank), F32),
            pltpu.VMEM((cells, rank), BF16),
            pltpu.VMEM((chunk, rank), BF16),
            pltpu.VMEM((cells, width), BF16),
            pltpu.VMEM((2, cells, width), BF16),
            pltpu.VMEM((cells, width), BF16),
            pltpu.VMEM((2, cells, width), BF16),
            pltpu.VMEM((2, cells, width), BF16),
            pltpu.VMEM((rank, cells), BF16),
            pltpu.VMEM((half, 2 * cells), BF16),
            pltpu.VMEM((9 * half, 2 * cells), BF16),
            pltpu.VMEM((2, rank, width), F32),
            pltpu.VMEM((2, rank, width), F32),
            pltpu.SemaphoreType.DMA((9,)),
            pltpu.SemaphoreType.DMA((6,)),
            pltpu.SemaphoreType.DMA((8,)),
            pltpu.SemaphoreType.DMA((8,)),
            pltpu.SemaphoreType.DMA((3, groups)),
            pltpu.SemaphoreType.DMA((3, groups)),
        ],
        compiler_params=pltpu.CompilerParams(
            collective_id=0, has_side_effects=True, vmem_limit_bytes=56 * 1024 * 1024
        ),
    )(
        activations.reshape(cells, channels),
        cotangent.reshape(cells, channels),
        kernel_taps,
        table,
        sample_tenant,
        tenant_slot,
        weight,
    )
    picks = (slots[:, 0, :1] == jnp.arange(tenants, dtype=jnp.int32)[None, :]).astype(BF16)
    sums = jnp.einsum("dl,dkc->lkc", picks, pieces, preferred_element_type=F32).astype(BF16)
    return (
        block_out.reshape(activations.shape),
        sums[:, : 9 * half].reshape(down_table.shape),
        sums[:, 9 * half :],
    )


def solution(mesh):
    placed = (
        P("ten", "fsdp", None, None),
        P("ten", "fsdp", None, None),
        P(None, "fsdp", None, None),
        P(None, None, None, "fsdp", "ten"),
        P(None, None, "ten"),
        P("ten"),
        P(),
        P("ten"),
    )
    return jax.shard_map(
        local_pair if mesh.shape["fsdp"] == 2 else local,
        mesh=mesh,
        in_specs=placed,
        out_specs=(
            P("ten", "fsdp", None, None),
            P(None, None, None, "fsdp", "ten"),
            P(None, None, "ten"),
        ),
        check_vma=False,
    )
```
